32 devices in a mesh: groups: 2 (over x), ctx: 16 (over z, y, core).
Axes of the slice: x: 2, y: 2, z: 4, core: 2. Of those that a mesh axis runs over, the one named last changes fastest.
Arguments:
- projected: bfloat16 [3, 16384, 4096], P(None, ('groups', 'ctx')), parts along dimension 1, may hold values from -6 to 6
- conv_weight: float32 [3, 4, 4096], replicated, may hold values from -3 to 3
- level_codes: int32 [14, 32, 16384], P(None, None, ('groups', 'ctx')), parts along dimension 2, may hold values from 1 to 16
- out_gain: float32 [4096], replicated, may hold values from 0.25 to 1.75
Outputs:
- mixed: bfloat16 [16384, 4096], P(('groups', 'ctx')), parts along dimension 0
The draws below stay inside these ranges and needn't reach their ends.
There are 2 independent parts, one for each index of `groups`. The reference program is written for one: setup_inputs(seed, part) draws one part's arguments, and reference() takes and returns one part's arrays. A program takes and returns all parts, laid end to end along the dimension named above; an argument that names none is the same for every part. Nothing has to cross between parts.
Inputs may be any that keep to these rules, and one draw needn't show every extreme that they name: `level_codes`: numerators of the level coefficients, which are the values divided by 8.
All inputs are finite; a program needn't handle non-finite values.
Results may differ from the reference program's by a relative error of at most 0.007.
Values may be sent and summed in bfloat16 or wider, within the bound.
No kernel may reach another device: no remote copies, remote signals or barrier semaphores. Data moves between devices by JAX's collectives and lax.ppermute only.
A program may use at most 192 MiB of HBM per device.

```python
import jax
import jax.numpy as jnp
from jax import lax

H = 32
DH = 128
D = 4096
KW = 4
TOK_DEV = 512
TOK_BITS = 9
CTX_BITS = 4
LEVELS = 14
TOKENS = 8192
N_CTX = 16


def touch_ends(array, key, smallest, high):
    dims = array.shape
    index_at = [jax.random.randint(jax.random.fold_in(key, axis), (), 0, dims[axis]) for axis in range(len(dims))]
    array = array.at[tuple(index_at)].set(smallest)
    longest = dims.index(max(dims))
    index_at[longest] = (index_at[longest] + 1) % dims[longest]
    return array.at[tuple(index_at)].set(high)


def levels(key, shape, pieces, least, high):
    factor_of, own = 1.0, jax.random.fold_in(key, 6)
    for dim, shards_of in pieces:
        draws = jnp.exp(jax.random.uniform(jax.random.fold_in(own, dim), (shards_of,), jnp.float32, least / len(pieces), high / len(pieces)))
        factor_of = factor_of * jnp.repeat(draws, shape[dim] // shards_of).reshape([-1 if axis == dim else 1 for axis in range(len(shape))])
    return factor_of


def noise(stream_key, dims, spread, limit, split=(), dtype=jnp.bfloat16):
    result = jax.random.normal(stream_key, dims, jnp.float32) * spread
    if len(split) > 0:
        result = levels(stream_key, dims, split, -0.22, 0.18) * result
    return jnp.clip(result, min=-limit, max=limit).astype(dtype)


def setup_inputs(seed: int = 0, part: int = 0) -> dict:
    splits = jax.random.split(jax.random.key(seed), 5)
    own_keys = jax.random.split(jax.random.fold_in(splits[4], part), 5)
    return {
        "projected": noise(own_keys[0], (3, TOKENS, D), 1.0, 6.0, ((1, 16),)),
        "conv_weight": noise(splits[1], (3, KW, D), 0.5, 3.0, (), jnp.float32),
        "level_codes": touch_ends(jax.random.randint(own_keys[2], (LEVELS, H, TOKENS), 1, 17), jax.random.fold_in(own_keys[2], 1), 1, 16).astype(jnp.int32),
        "out_gain": jnp.clip(1.0 + 0.15 * jax.random.normal(splits[3], (D,), jnp.float32), 0.25, 1.75),
    }


def convolve(projected, conv_weight):
    tap_count = conv_weight.shape[1]
    row_count = projected.shape[1]
    source = projected.astype(jnp.float32)
    padded = jnp.concatenate([jnp.zeros((3, tap_count - 1, source.shape[2]), jnp.float32), source], 1)
    running = jnp.zeros(source.shape, jnp.float32)
    for offset in range(tap_count):
        running = running + conv_weight[:, offset, None, :] * padded[:, offset:offset + row_count, :]
    return running.astype(jnp.bfloat16)

def intra_levels(length, bit_count):
    position = lax.iota(jnp.int32, length)
    differ = jnp.bitwise_xor(position[:, None], position[None, :])
    level = jnp.zeros((length, length), jnp.int32)
    for exponent in range(bit_count):
        level = level + (differ >= 2 ** exponent).astype(jnp.int32)
    causal = position[None, :] <= position[:, None]
    return jnp.stack([(causal & (level == number)).astype(jnp.float32) for number in range(bit_count + 1)])

def local_layer(query_rows, key_rows, value_rows, level_weight, fenwick, onehot, out_gain):
    highest = lax.Precision.HIGHEST
    scores = jnp.einsum('thd,shd->hts', query_rows, key_rows, precision=highest)
    weight = jnp.einsum('lts,lht->hts', onehot, level_weight[:TOK_BITS + 1], precision=highest)
    weights = lax.optimization_barrier((scores * weight).astype(jnp.bfloat16)).astype(jnp.float32)
    inside = jnp.einsum('hts,shd->thd', weights, value_rows, precision=highest)
    fenwick_bf = lax.optimization_barrier(fenwick.astype(jnp.bfloat16)).astype(jnp.float32)
    across = jnp.zeros(inside.shape, jnp.float32)
    for bit_index in range(CTX_BITS):
        product = jnp.einsum('thd,hde->the', query_rows, fenwick_bf[bit_index], precision=highest)
        across = across + level_weight[TOK_BITS + 1 + bit_index].T[:, :, None] * product
    combined = inside + across
    inverse = lax.rsqrt(lax.optimization_barrier(jnp.mean(combined * combined, -1, keepdims=True)) + 1e-06)
    normed = combined * inverse * out_gain.reshape(H, DH)
    return normed.astype(jnp.bfloat16).reshape(TOK_DEV, H * DH)

def reference(projected, conv_weight, level_codes, out_gain):
    mixed_in = convolve(projected, conv_weight)
    level_weight = level_codes.astype(jnp.float32) / 8.0
    onehot = intra_levels(TOK_DEV, TOK_BITS)
    heads_all = mixed_in.reshape(3, N_CTX, TOK_DEV, H, DH).astype(jnp.float32)
    states = jnp.einsum('cshd,cshe->chde', heads_all[1], heads_all[2], precision=lax.Precision.HIGHEST)
    span_ids = lax.iota(jnp.int32, N_CTX)
    differ = jnp.bitwise_xor(span_ids[:, None], span_ids[None, :])
    earlier = span_ids[None, :] < span_ids[:, None]
    bucket_masks = jnp.stack([(earlier & (differ >= 2 ** bit_index) & (differ < 2 ** (bit_index + 1))).astype(jnp.float32) for bit_index in range(CTX_BITS)])
    outputs = []
    for span_index in range(N_CTX):
        fenwick = jnp.einsum('bs,shde->bhde', bucket_masks[:, span_index, :], states, precision=lax.Precision.HIGHEST)
        level_part = level_weight[:, :, span_index * TOK_DEV:(span_index + 1) * TOK_DEV]
        outputs.append(local_layer(heads_all[0, span_index], heads_all[1, span_index], heads_all[2, span_index], level_part, fenwick, onehot, out_gain))
    return jnp.concatenate(outputs, 0)
```

```python
import functools

import jax
import jax.numpy as jnp
from jax import lax
from jax.experimental import pallas as pl
from jax.experimental.pallas import tpu as pltpu
from jax.sharding import PartitionSpec as P

NT = (((1,), (1,)), ((), ()))
ROOM = 56 * 1024 * 1024


def convolve(x_ref, rim_ref, w_ref, pad_ref, emit):
    rows, width = x_ref.shape
    taps = w_ref.shape[0]
    base = pad_ref.shape[0] - rows
    step = min(64, rows)
    pad_ref[base - (taps - 1) : base, :] = rim_ref[...].astype(jnp.float32)
    for row in range(0, rows, step):
        pad_ref[base + row : base + row + step, :] = x_ref[row : row + step, :].astype(jnp.float32)
    for col in range(0, width, 128):
        w = w_ref[:, col : col + 128]
        for row in range(0, rows, step):
            total = None
            for tap in range(taps):
                at = base - (taps - 1) + tap + row
                term = w[tap : tap + 1, :] * pad_ref[at : at + step, col : col + 128]
                total = term if total is None else total + term
            emit(row, col, total)


def kv_kernel(place, xk, xv, rk, rv, wk, wv, k_out, vt_out, s_out, padk, padv, vrow):
    rows = xk.shape[0]
    heads, dim = vt_out.shape[0], vt_out.shape[1]

    def emit_k(row, col, total):
        k_out[row : row + total.shape[0], col : col + 128] = total.astype(jnp.bfloat16)

    def emit_v(row, col, total):
        vrow[row : row + total.shape[0], col : col + 128] = total.astype(jnp.bfloat16)

    convolve(xk, rk, wk, padk, emit_k)
    convolve(xv, rv, wv, padv, emit_v)
    for head in range(heads):
        cols = slice(head * dim, (head + 1) * dim)
        vt = vrow[:, cols].T
        vt_out[head] = vt
        s_out[head] = jnp.dot(vt, k_out[:, cols], preferred_element_type=jnp.float32).astype(
            s_out.dtype
        )


def inner_weights(lam, block):
    rows = lam[0].shape[1]
    lane = lax.broadcasted_iota(jnp.int32, (8, rows), 1)
    sub = lax.broadcasted_iota(jnp.int32, (8, rows), 0)
    zero = jnp.zeros((8, rows), jnp.float32)
    near = zero
    differ = (lane & 7) ^ sub
    for level in range(1, 4):
        near = jnp.where((differ >> (level - 1)) == 1, lam[level], near)
    near = jnp.where(differ == 0, lam[0], near)
    near = jnp.where(sub <= (lane & 7), near, zero)
    group = (lane >> 3) & (block // 8 - 1)
    out = []
    for first in range(0, block // 8, 8):
        index = sub + first
        apart = index ^ group
        far = zero
        for level in range(4, block.bit_length()):
            far = jnp.where((apart >> (level - 4)) == 1, lam[level], far)
        far = jnp.where(index < group, far, zero)
        for i in range(8):
            wide = jnp.broadcast_to(far[i : i + 1, :], (8, rows))
            out.append(jnp.where(group == first + i, near, wide))
    return out


def inside_kernel(place, xq, rq, wq, k_in, vt_in, codes, q_out, in_out, padq, p_ref):
    rows = xq.shape[0]
    heads, dim = vt_in.shape[0], vt_in.shape[1]
    block = min(128, rows)
    wide = min(256, rows)
    levels = codes.shape[0]
    bits = rows.bit_length() - 1

    def emit_q(row, col, total):
        q_out[row : row + total.shape[0], col : col + 128] = total.astype(jnp.bfloat16)

    convolve(xq, rq, wq, padq, emit_q)
    for head in range(heads):
        cols = slice(head * dim, (head + 1) * dim)
        at = lax.rem(place[1] + pl.program_id(0) * heads + head, codes.shape[1])
        lam = [codes[level, pl.ds(at, 1), :].astype(jnp.float32) * 0.125 for level in range(bits + 1)]
        near = inner_weights(lam, block)
        for first in range(0, rows, wide):
            reach = first + wide
            scores = lax.dot_general(
                k_in[0:reach, cols],
                q_out[first : first + wide, cols],
                NT,
                preferred_element_type=jnp.float32,
            )
            for t0 in range(first, reach, block):
                span = slice(t0 - first, t0 - first + block)
                for s0 in range(0, reach, block):
                    if s0 > t0:
                        p_ref[head, s0 : s0 + block, t0 : t0 + block] = jnp.zeros(
                            (block, block), jnp.bfloat16
                        )
                        continue
                    if s0 == t0:
                        weight = jnp.concatenate([n[:, t0 : t0 + block] for n in near], 0)
                    else:
                        level = (s0 ^ t0).bit_length()
                        weight = lam[level][:, t0 : t0 + block]
                    part = scores[s0 : s0 + block, span] * weight
                    p_ref[head, s0 : s0 + block, t0 : t0 + block] = part.astype(jnp.bfloat16)
            in_out[head, :, first:reach] = jnp.dot(
                vt_in[head, :, 0:reach],
                p_ref[head, 0:reach, first:reach],
                preferred_element_type=jnp.float32,
            )


def across_kernel(bits, inner, place, q_in, in_in, codes, gain, *rest):
    states, out = rest[:bits], rest[-1]
    heads, dim, rows = in_in.shape
    for head in range(heads):
        cols = slice(head * dim, (head + 1) * dim)
        at = lax.rem(place[1] + pl.program_id(0) * heads + head, codes.shape[1])
        q = q_in[:, cols]
        total = in_in[head]
        for bit in range(bits):
            scale = place[3 + bit].astype(jnp.float32) * 0.125
            lam = codes[inner + bit, pl.ds(at, 1), :].astype(jnp.float32) * scale
            part = lax.dot_general(states[bit][head], q, NT, preferred_element_type=jnp.float32)
            total = total + lam * part
        mean = jnp.sum(total * total, 0, keepdims=True) * (1.0 / dim)
        normed = total * lax.rsqrt(mean + 1e-06)
        out[:, cols] = (normed.T * gain[:, cols]).astype(jnp.bfloat16)


def on_device(projected, conv_weight, level_codes, out_gain):
    taps = conv_weight.shape[1]
    rows, width = projected.shape[1:]
    levels, head_count = level_codes.shape[:2]
    dim = width // head_count
    tok_bits = rows.bit_length() - 1
    count = lax.axis_size("ctx")
    bits = count.bit_length() - 1
    index = lax.axis_index("ctx")
    core, side = index & 1, (index >> 1) & 1
    half, quarter = head_count // 2, head_count // 4
    group = 2
    code_rows = min(8, head_count)
    flags = [(index >> bit) & 1 for bit in range(bits)]
    gain = out_gain.reshape(1, width)

    def exchange(value, bit):
        return lax.ppermute(value, "ctx", [(i, i ^ (1 << bit)) for i in range(count)])

    rim = lax.ppermute(
        projected[:, rows - taps + 1 :, :], "ctx", [(i, i + 1) for i in range(count - 1)]
    )

    def place(head, local):
        return jnp.stack([head // group, head, local // group] + flags).astype(jnp.int32)

    def third(which, size):
        return pl.BlockSpec((None, size, group * dim), lambda i, p: (which, 0, p[0] + i))

    def per_head(*shape):
        return pl.BlockSpec((group, *shape), lambda i, p: (i, 0, 0))

    column = pl.BlockSpec((rows, group * dim), lambda i, p: (0, i))
    code_spec = pl.BlockSpec(
        (levels, code_rows, rows), lambda i, p: (0, (p[1] + i * group) // code_rows, 0)
    )
    params = pltpu.CompilerParams(vmem_limit_bytes=ROOM)
    pad = pltpu.VMEM((rows + 8, group * dim), jnp.float32)
    bf16, f32 = jnp.bfloat16, jnp.float32

    def key_value(head, count_heads):
        return pl.pallas_call(
            kv_kernel,
            grid_spec=pltpu.PrefetchScalarGridSpec(
                num_scalar_prefetch=1,
                grid=(count_heads // group,),
                in_specs=[
                    third(1, rows),
                    third(2, rows),
                    third(1, taps - 1),
                    third(2, taps - 1),
                    third(1, taps),
                    third(2, taps),
                ],
                out_specs=[column, per_head(dim, rows), per_head(dim, dim)],
                scratch_shapes=[pad, pad, pltpu.VMEM((rows, group * dim), bf16)],
            ),
            out_shape=[
                jax.ShapeDtypeStruct((rows, count_heads * dim), bf16),
                jax.ShapeDtypeStruct((count_heads, dim, rows), bf16),
                jax.ShapeDtypeStruct((count_heads, dim, dim), bf16),
            ],
            compiler_params=params,
            name="key_value",
        )(place(head, head * 0), projected, projected, rim, rim, conv_weight, conv_weight)

    def inside(head, keys, values):
        count_heads = values.shape[0]
        return pl.pallas_call(
            inside_kernel,
            grid_spec=pltpu.PrefetchScalarGridSpec(
                num_scalar_prefetch=1,
                grid=(count_heads // group,),
                in_specs=[
                    third(0, rows),
                    third(0, taps - 1),
                    third(0, taps),
                    column,
                    per_head(dim, rows),
                    code_spec,
                ],
                out_specs=[column, per_head(dim, rows)],
                scratch_shapes=[pad, pltpu.VMEM((group, rows, rows), bf16)],
            ),
            out_shape=[
                jax.ShapeDtypeStruct((rows, count_heads * dim), bf16),
                jax.ShapeDtypeStruct((count_heads, dim, rows), f32),
            ],
            compiler_params=params,
            name="inside",
        )(place(head, head * 0), projected, rim, conv_weight, keys, values, level_codes)

    def across(head, local, queries, inner, states, out):
        count_heads = states[0][0].shape[0] if isinstance(states[0], tuple) else states[0].shape[0]
        arrays, specs = [], []
        for state in states:
            if isinstance(state, tuple):
                arrays.append(state[0])
                specs.append(pl.BlockSpec((group, dim, dim), lambda i, p: (p[2] + i, 0, 0)))
                count_heads = quarter
            else:
                arrays.append(state)
                specs.append(pl.BlockSpec((group, dim, dim), lambda i, p: (i, 0, 0)))
        extra = [] if out is None else [out]
        return pl.pallas_call(
            functools.partial(across_kernel, bits, tok_bits + 1),
            grid_spec=pltpu.PrefetchScalarGridSpec(
                num_scalar_prefetch=1,
                grid=(quarter // group,),
                in_specs=[
                    pl.BlockSpec((rows, group * dim), lambda i, p: (0, p[2] + i)),
                    pl.BlockSpec((group, dim, rows), lambda i, p: (p[2] + i, 0, 0)),
                    code_spec,
                    pl.BlockSpec((1, group * dim), lambda i, p: (0, p[0] + i)),
                ]
                + specs
                + [pl.BlockSpec(memory_space=pl.ANY)] * len(extra),
                out_specs=pl.BlockSpec((rows, group * dim), lambda i, p: (0, p[0] + i)),
            ),
            out_shape=jax.ShapeDtypeStruct((rows, width), bf16),
            input_output_aliases={} if out is None else {5 + bits: 0},
            compiler_params=params,
            name="across",
        )(place(head, local), queries, inner, level_codes, gain, *arrays, *extra)

    other_head, own_head = (1 - core) * half, core * half
    near, far = side * quarter, (1 - side) * quarter

    def part(value, start):
        return lax.dynamic_slice_in_dim(value, start, quarter, 0)

    other_k, other_v, other_s = key_value(other_head, half)
    got0 = exchange(other_s, 0)
    own_k, own_v, own_s = key_value(own_head, half)
    total = own_s + got0
    near1 = exchange(part(total, far), 1)
    running = part(total, near) + near1
    far1 = exchange(part(total, near), 1)
    got0_other = exchange(own_s, 0)
    own_q, own_in = inside(own_head, own_k, own_v)
    other_q, other_in = inside(other_head, other_k, other_v)
    nears, fars = [near1], [far1]
    for bit in range(2, bits):
        ones = (1 << bit) - 4
        got = None
        for low in range(1 << (bit - 2)):
            pairs = [
                (i, (i & ~ones) | (low << 2) | (1 << bit))
                for i in range(count)
                if i & ones == ones and not i >> bit & 1
            ]
            piece = lax.ppermute(running, "ctx", pairs)
            got = piece if got is None else got + piece
        running = running + got
        nears.append(got)
        fars.append(exchange(got, 1))
    other_nears = [exchange(value, 0) for value in nears]
    other_fars = [exchange(value, 0) for value in fars]
    out = across(own_head + near, near, own_q, own_in, [(got0,)] + nears, None)
    out = across(other_head + near, near, other_q, other_in, [(got0_other,)] + other_nears, out)
    out = across(own_head + far, far, own_q, own_in, [(got0,)] + fars, out)
    out = across(other_head + far, far, other_q, other_in, [(got0_other,)] + other_fars, out)
    return out


def solution(mesh):
    placed = (P(None, ("groups", "ctx"), None), P(), P(None, None, ("groups", "ctx")), P())
    return jax.shard_map(
        on_device, mesh=mesh, in_specs=placed, out_specs=P(("groups", "ctx"), None), check_vma=False
    )
```

```python
import functools

import jax
import jax.numpy as jnp
from jax import lax
from jax.experimental import pallas as pl
from jax.experimental.pallas import tpu as pltpu
from jax.sharding import PartitionSpec as P

NT = (((1,), (1,)), ((), ()))
ROOM = 8 * 1024 * 1024
GROUP = 8
VMEM = pltpu.VMEM


def lanes(head, dim):
    return pl.ds(pl.multiple_of(head * dim, dim), dim)


def base_of(place, where, heads):
    index = place[0]
    return (((index & 1) ^ where[0]) * 2 + (((index >> 1) & 1) ^ where[1])) * heads


def convolve(x, at, rim, w, which, head, dim, step=128):
    rows, taps = x.shape[1], w.shape[1]
    cols = lanes(head, dim)
    w_rows = [w[which, tap : tap + 1, cols] for tap in range(taps)]
    before = jnp.concatenate(
        [jnp.zeros((9 - taps, dim), jnp.float32), rim[which, :, cols].astype(jnp.float32)], 0
    )
    out = []
    for row in range(0, rows, step):
        chunk = x[at, row : row + step, cols].astype(jnp.float32)
        full = jnp.concatenate([before, chunk], 0)
        total = None
        for tap in range(taps - 2, -1, -2):
            pair = w_rows[tap + 1] * full + w_rows[tap] * pltpu.roll(full, 1, 0)
            if tap < taps - 2:
                pair = pltpu.roll(pair, taps - 2 - tap, 0)
            total = pair if total is None else total + pair
        out.append(total[8:].astype(jnp.bfloat16))
        before = chunk[step - 8 :]
    return jnp.concatenate(out, 0)


def kv_kernel(first, merge, extra, where, place, rim, w, x, *rest):
    rest, sems = rest[:-1], rest[-1]
    copies, arrivals = [], {}
    if first:
        code_home, gain_home, *rest = rest
        k_out, vt_out, s_out, x_in, xq, codes, gain, w_in = rest
        home, x, w_home, w = x, x_in, w, w_in
        heads, dim = vt_out.shape[:2]
        base = base_of(place, where, heads)
        head_count = x.shape[2] // dim
        width = GROUP * dim

        def bring(source, target):
            copy = pltpu.make_async_copy(source, target, sems.at[len(copies)])
            copy.start()
            copies.append(copy)
            return copy

        arrivals[0] = [bring(w_home, w)]
        for step in range(heads // GROUP):
            cols = pl.ds(pl.multiple_of((base + step * GROUP) * dim, width), width)
            arrivals[step] = arrivals.get(step, []) + [
                bring(home.at[which, :, cols], x.at[which - 1, :, cols]) for which in (1, 2)
            ]
        for other in range(1, head_count // heads):
            head = lax.rem(base + other * heads, head_count)
            cols = pl.ds(pl.multiple_of(head * dim, heads * dim), heads * dim)
            for which in (1, 2):
                bring(home.at[which, :, cols], x.at[which - 1, :, cols])
        bring(home.at[0], xq.at[0])
        bring(code_home, codes)
        bring(gain_home, gain)
    elif merge:
        got_home, k_out, vt_out, s_out, sum_out, got = rest
        copies.append(pltpu.make_async_copy(got_home, got, sems.at[0]))
        copies[0].start()
    else:
        k_out, vt_out, s_out = rest[extra:]
    heads, dim = vt_out.shape[:2]
    base = base_of(place, where, heads)

    for step in range(heads // GROUP):
        for copy in arrivals.get(step, []):
            copy.wait()
    if merge:
        copies[0].wait()

    @pl.loop(0, heads // GROUP)
    def _(step):
        for unit in range(GROUP):
            head = step * GROUP + unit
            keys = convolve(x, 0, rim, w, 1, base + head, dim)
            k_out[:, lanes(head, dim)] = keys
            vt = convolve(x, 1, rim, w, 2, base + head, dim).T
            vt_out[head] = vt
            state = jnp.dot(vt, keys, preferred_element_type=jnp.float32)
            s_out[head] = state.astype(jnp.bfloat16)
            if merge:
                sum_out[head] = (state + got[head].astype(jnp.float32)).astype(jnp.bfloat16)

    if first:
        for copy in copies[2 * (heads // GROUP) + 1 :]:
            copy.wait()


def merge_kernel(*refs):
    count = refs[-1].shape[0]
    out, held, sems = refs[-4], refs[-3], refs[-1]
    copies = [pltpu.make_async_copy(refs[i], held.at[i], sems.at[i]) for i in range(count)]
    for copy in copies:
        copy.start()
    for copy in copies:
        copy.wait()
    total = held[0].astype(jnp.float32)
    for i in range(1, count):
        total = total + held[i].astype(jnp.float32)
    refs[-2][...] = total.astype(refs[-2].dtype)
    last = pltpu.make_async_copy(refs[-2], out, sems.at[0])
    last.start()
    last.wait()


def inner_weights(lam, block):
    rows = lam[0].shape[1]
    lane = lax.broadcasted_iota(jnp.int32, (8, rows), 1)
    sub = lax.broadcasted_iota(jnp.int32, (8, rows), 0)
    zero = jnp.zeros((8, rows), jnp.float32)
    near = zero
    differ = (lane & 7) ^ sub
    for level in range(1, 4):
        near = jnp.where((differ >> (level - 1)) == 1, lam[level], near)
    near = jnp.where(differ == 0, lam[0], near)
    near = jnp.where(sub <= (lane & 7), near, zero)
    group = (lane >> 3) & (block // 8 - 1)
    out = []
    for first in range(0, block // 8, 8):
        index = sub + first
        apart = index ^ group
        far = zero
        for level in range(4, block.bit_length()):
            far = jnp.where((apart >> (level - 4)) == 1, lam[level], far)
        far = jnp.where(index < group, far, zero)
        for i in range(8):
            wide = jnp.broadcast_to(far[i : i + 1, :], (8, rows))
            out.append(jnp.where(group == first + i, near, wide))
    return out


def pack_kernel(count, *refs):
    out, sems = refs[-2:]
    copies = [pltpu.make_async_copy(refs[i], out.at[i], sems.at[i]) for i in range(count)]
    for copy in copies:
        copy.start()
    for copy in copies:
        copy.wait()


def inside_kernel(where, place, x, rim, w, k_in, vt_in, codes, after, q_out, in_out):
    rows = x.shape[1]
    heads, dim = vt_in.shape[:2]
    base = base_of(place, where, heads)
    block, wide = min(128, rows), min(256, rows)
    bits = rows.bit_length() - 1

    @pl.loop(0, heads // GROUP)
    def _(step):
        for unit in range(GROUP):
            head = step * GROUP + unit
            cols = lanes(head, dim)
            queries = convolve(x, 0, rim, w, 0, base + head, dim)
            q_out[:, cols] = queries
            lam = [
                codes[level, pl.ds(base + head, 1), :].astype(jnp.float32) * 0.125
                for level in range(bits + 1)
            ]
            near = inner_weights(lam, block)
            for first in range(0, rows, wide):
                reach = first + wide
                scores = lax.dot_general(
                    k_in[0:reach, cols],
                    queries[first:reach],
                    NT,
                    preferred_element_type=jnp.float32,
                )
                columns = []
                for t0 in range(first, reach, block):
                    span = slice(t0 - first, t0 - first + block)
                    parts = []
                    for s0 in range(0, reach, block):
                        if s0 > t0:
                            parts.append(jnp.zeros((block, block), jnp.bfloat16))
                            continue
                        if s0 == t0:
                            weight = jnp.concatenate([n[:, t0 : t0 + block] for n in near], 0)
                        else:
                            weight = lam[(s0 ^ t0).bit_length()][:, t0 : t0 + block]
                        parts.append((scores[s0 : s0 + block, span] * weight).astype(jnp.bfloat16))
                    columns.append(jnp.concatenate(parts, 0))
                in_out[head, :, first:reach] = jnp.dot(
                    vt_in[head, :, 0:reach],
                    jnp.concatenate(columns, 1),
                    preferred_element_type=jnp.float32,
                )


def across_kernel(bits, inner, held, where, slots, place, q_in, in_in, codes, gain, *rest):
    states, out, token = rest[:bits], rest[bits + held], rest[bits + held + 1]
    fen, mixed, sems = rest[bits + held + 2 :]
    token[...] = jnp.zeros_like(token)
    heads, dim, rows = in_in.shape
    base = base_of(place, where, heads)
    copies = [
        pltpu.make_async_copy(
            states[bit] if slots[bit] is None else states[bit].at[slots[bit]],
            fen.at[:, bit * dim : (bit + 1) * dim, :],
            sems.at[bit],
        )
        for bit in range(bits)
    ]
    for copy in copies:
        copy.start()
    for copy in copies:
        copy.wait()
    scales = [((place[0] >> bit) & 1).astype(jnp.float32) * 0.125 for bit in range(bits)]
    wide = min(256, rows)

    @pl.loop(0, heads // GROUP)
    def _(step):
        for unit in range(GROUP):
            head = step * GROUP + unit
            cols = lanes(head, dim)
            lam = [
                codes[inner + bit, pl.ds(base + head, 1), :].astype(jnp.float32) * scales[bit]
                for bit in range(bits)
            ]
            for t0 in range(0, rows, wide):
                span = slice(t0, t0 + wide)
                parts = lax.dot_general(
                    fen[head], q_in[span, cols], NT, preferred_element_type=jnp.float32
                )
                total = in_in[head, :, span]
                for bit in range(bits):
                    total = total + lam[bit][:, span] * parts[bit * dim : (bit + 1) * dim]
                mean = jnp.sum(total * total, 0, keepdims=True) * (1.0 / dim)
                normed = total * lax.rsqrt(mean + 1e-06)
                mixed[span, cols] = (normed.T * gain[:, lanes(base + head, dim)]).astype(
                    jnp.bfloat16
                )

    width = heads * dim
    home = out.at[:, pl.ds(pl.multiple_of(base * dim, width), width)]
    last = pltpu.make_async_copy(mixed, home, sems.at[bits])
    last.start()
    last.wait()


def on_device(projected, conv_weight, level_codes, out_gain):
    taps = conv_weight.shape[1]
    rows, width = projected.shape[1:]
    levels, head_count = level_codes.shape[:2]
    dim = width // head_count
    tok_bits = rows.bit_length() - 1
    count = lax.axis_size("ctx")
    bits = count.bit_length() - 1
    index = lax.axis_index("ctx")
    quarter = head_count // 4
    bf16, f32 = jnp.bfloat16, jnp.float32

    def exchange(value, bit):
        return lax.ppermute(value, "ctx", [(i, i ^ (1 << bit)) for i in range(count)])

    rim = lax.ppermute(
        projected[:, rows - taps + 1 :, :], "ctx", [(i, i + 1) for i in range(count - 1)]
    )

    def kept(value):
        return pltpu.with_memory_space_constraint(value, VMEM)

    place = index.reshape(1).astype(jnp.int32)
    params = pltpu.CompilerParams(vmem_limit_bytes=ROOM)
    whole = pl.BlockSpec(memory_space=VMEM)
    scalars = pl.BlockSpec(memory_space=pltpu.SMEM)
    anywhere = pl.BlockSpec(memory_space=pl.ANY)
    state = jax.ShapeDtypeStruct((quarter, dim, dim), bf16)

    def key_value(where, source, weight, first=False, got=None, after=None):
        merge, extra = got is not None, 0 if after is None else 1
        made = [VMEM((rows, quarter * dim), bf16), VMEM((quarter, dim, rows), bf16), state]
        scratch, operands = [], [place, rim, weight, source]
        specs = [scalars, whole] + [anywhere if first else whole] * 2
        if first:
            gain = out_gain.reshape(1, width)
            operands[-2:] = [
                pltpu.with_memory_space_constraint(a, pltpu.HBM)
                for a in (weight, source, level_codes, gain)
            ]
            specs += [anywhere] * 2
            made += [VMEM((2, rows, width), bf16), VMEM((1, rows, width), bf16)]
            made += [VMEM(a.shape, a.dtype) for a in (level_codes, gain, weight)]
        if merge:
            operands.append(got)
            specs.append(anywhere)
            made.append(state)
            scratch.append(VMEM(state.shape, bf16))
        if extra:
            operands.append(after)
            specs.append(anywhere)
        return pl.pallas_call(
            functools.partial(kv_kernel, first, merge, extra, where),
            in_specs=specs,
            out_specs=[whole] * len(made),
            out_shape=made,
            scratch_shapes=scratch + [pltpu.SemaphoreType.DMA((2 * quarter // GROUP + 10,))],
            compiler_params=params,
            name="key_value",
        )(*operands)

    def merged(values, after):
        return pl.pallas_call(
            merge_kernel,
            in_specs=[anywhere] * (len(values) + len(after)),
            out_specs=anywhere,
            out_shape=state,
            scratch_shapes=[
                VMEM((len(values), *state.shape), bf16),
                VMEM(state.shape, bf16),
                pltpu.SemaphoreType.DMA((len(values),)),
            ],
            compiler_params=params,
            name="merge",
        )(*values, *after)

    def packed(values, after):
        shape = (len(values), *state.shape)
        return pl.pallas_call(
            functools.partial(pack_kernel, len(values)),
            in_specs=[anywhere] * (len(values) + len(after)),
            out_specs=anywhere,
            out_shape=jax.ShapeDtypeStruct(shape, bf16),
            scratch_shapes=[pltpu.SemaphoreType.DMA((len(values),))],
            compiler_params=params,
            name="pack",
        )(*values, *after)

    def inside(where, after):
        return pl.pallas_call(
            functools.partial(inside_kernel, where),
            in_specs=[scalars] + [whole] * 6 + [anywhere],
            out_specs=[whole] * 2,
            out_shape=[VMEM((rows, quarter * dim), bf16), VMEM((quarter, dim, rows), f32)],
            compiler_params=params,
            name="inside",
        )(
            place, raw, rim, weight, kept(keys[where]), kept(values[where]), codes, after
        )

    def across(where, local, states, out):
        held = [] if out is None else [out]
        queries, inner = local
        states, slots = zip(*(a if isinstance(a, tuple) else (a, None) for a in states))
        return pl.pallas_call(
            functools.partial(across_kernel, bits, tok_bits + 1, len(held), where, slots),
            in_specs=[scalars] + [whole] * 4 + [anywhere] * (bits + len(held)),
            out_specs=[anywhere, whole],
            out_shape=[jax.ShapeDtypeStruct((rows, width), bf16), VMEM((8, 128), f32)],
            input_output_aliases={5 + bits: 0} if held else {},
            scratch_shapes=[
                VMEM((quarter, bits * dim, dim), bf16),
                VMEM((rows, quarter * dim), bf16),
                pltpu.SemaphoreType.DMA((bits + 1,)),
            ],
            compiler_params=params,
            name="across",
        )(place, kept(queries), kept(inner), codes, gain, *states, *held)

    near, far, other_near, other_far = (0, 0), (0, 1), (1, 0), (1, 1)
    keys, values, local = {}, {}, {}
    keys[other_far], values[other_far], sent, source, raw, codes, gain, weight = key_value(
        other_far, projected, conv_weight, first=True
    )
    source, raw, codes, gain, weight = map(kept, (source, raw, codes, gain, weight))
    got_far = exchange(sent, 0)
    keys[far], values[far], state_far, total_far = key_value(far, source, weight, got=got_far)
    near1 = exchange(total_far, 1)
    keys[other_near], values[other_near], sent = key_value(
        other_near, source, weight, after=total_far
    )
    got_near = exchange(sent, 0)
    keys[near], values[near], state_near, total_near = key_value(
        near, source, weight, got=got_near
    )
    far1 = exchange(total_near, 1)
    nears, fars = [got_near, near1], [got_far, far1]
    running = merged([total_near, near1], [])
    waiting = [near, far, other_near, other_far]

    def work(where, after):
        waiting.remove(where)
        local[where] = inside(where, after)
        return local[where][1]

    for bit in range(2, bits):
        ones = (1 << bit) - 4
        pieces = []
        for low in reversed(range(1 << (bit - 2))):
            pairs = [
                (i, (i & ~ones) | (low << 2) | (1 << bit))
                for i in range(count)
                if i & ones == ones and not i >> bit & 1
            ]
            pieces.append(lax.ppermute(running, "ctx", pairs))
        after = []
        for _ in range(bit - 1):
            if len(waiting) > 1:
                after.append(work(waiting[0], after[-1] if after else running))
        got = merged(pieces, after) if len(pieces) > 1 else pieces[0]
        if bit + 1 < bits:
            running = merged([running, got], after)
        nears.append(got)
        fars.append(exchange(got, 1))
        if bit == 2:
            early = exchange(packed([state_near, near1, state_far, far1], [running]), 0)
    late = exchange(packed(nears[2:] + fars[2:-1], []), 0)
    after = [work(where, nears[-1]) for where in list(waiting)]
    out, token = across(near, local[near], nears, None)
    last = merged(fars[-1:], after + [token])
    later = bits - 2
    other_nears = [(early, 0), (early, 1)] + [(late, i) for i in range(later)]
    other_fars = [(early, 2), (early, 3)] + [(late, later + i) for i in range(later - 1)]
    other_fars.append(exchange(last, 0))
    out, _ = across(other_near, local[other_near], other_nears, out)
    out, _ = across(far, local[far], fars[:-1] + [last], out)
    return across(other_far, local[other_far], other_fars, out)[0]


def solution(mesh):
    placed = (P(None, ("groups", "ctx"), None), P(), P(None, None, ("groups", "ctx")), P())
    return jax.shard_map(
        on_device, mesh=mesh, in_specs=placed, out_specs=P(("groups", "ctx"), None), check_vma=False
    )
```

```python
import functools

import jax
import jax.numpy as jnp
from jax import lax
from jax.experimental import pallas as pl
from jax.experimental.pallas import tpu as pltpu
from jax.sharding import PartitionSpec as P

NT = (((1,), (1,)), ((), ()))
ROOM = 8 * 1024 * 1024
GROUP = 8
VMEM = pltpu.VMEM


def lanes(head, dim):
    return pl.ds(pl.multiple_of(head * dim, dim), dim)


def base_of(place, where, heads):
    index = place[0]
    return (((index & 1) ^ where[0]) * 2 + (((index >> 1) & 1) ^ where[1])) * heads


def before_span(place, even, odd, which, cols):
    index = place[0]
    rows = jnp.where((index & 1) == 1, odd[which, :, cols], even[which, :, cols])
    return jnp.where(index == 0, 0.0, rows.astype(jnp.float32))


def convolve(x, at, place, even, odd, w, which, head, dim, step=128):
    rows, taps = x.shape[1], w.shape[1]
    cols = lanes(head, dim)
    w_rows = [w[which, tap : tap + 1, cols] for tap in range(taps)]
    before = jnp.concatenate(
        [jnp.zeros((9 - taps, dim), jnp.float32), before_span(place, even, odd, which, cols)], 0
    )
    out = []
    for row in range(0, rows, step):
        chunk = x[at, row : row + step, cols].astype(jnp.float32)
        full = jnp.concatenate([before, chunk], 0)
        total = None
        for tap in range(taps - 2, -1, -2):
            pair = w_rows[tap + 1] * full + w_rows[tap] * pltpu.roll(full, 1, 0)
            if tap < taps - 2:
                pair = pltpu.roll(pair, taps - 2 - tap, 0)
            total = pair if total is None else total + pair
        out.append(total[8:].astype(jnp.bfloat16))
        before = chunk[step - 8 :]
    return jnp.concatenate(out, 0)


def stage_kernel(count, first, *refs):
    outs, sems = refs[-1 - count : -1], refs[-1]
    copies = [
        pltpu.make_async_copy(home, out, sems.at[i])
        for i, (home, out) in enumerate(zip(refs, outs))
        if home.shape == out.shape
    ]
    if refs[0].shape != outs[0].shape:
        part = refs[0].at[first : first + outs[0].shape[0]]
        copies.append(pltpu.make_async_copy(part, outs[0], sems.at[0]))
    for copy in copies:
        copy.start()
    for copy in copies:
        copy.wait()


def kv_kernel(merge, extra, where, place, even, odd, w, x, *rest):
    if merge:
        got_home, rest, got, sems = rest[0], rest[1:-2], rest[-2], rest[-1]
        copy = pltpu.make_async_copy(got_home, got, sems.at[0])
        copy.start()
    rest = rest[extra:]
    k_out, vt_out, s_out = rest[:3]
    heads, dim = vt_out.shape[:2]
    base = base_of(place, where, heads)
    if merge:
        sum_out = rest[3]
        copy.wait()

    @pl.loop(0, heads // GROUP)
    def _(step):
        for unit in range(GROUP):
            head = step * GROUP + unit
            keys = convolve(x, 0, place, even, odd, w, 1, base + head, dim)
            k_out[:, lanes(head, dim)] = keys
            vt = convolve(x, 1, place, even, odd, w, 2, base + head, dim).T
            vt_out[head] = vt
            state = jnp.dot(vt, keys, preferred_element_type=jnp.float32)
            s_out[head] = state.astype(jnp.bfloat16)
            if merge:
                sum_out[head] = (state + got[head].astype(jnp.float32)).astype(jnp.bfloat16)


def merge_kernel(*refs):
    count = refs[-1].shape[0]
    out, held, sems = refs[-4], refs[-3], refs[-1]
    copies = [pltpu.make_async_copy(refs[i], held.at[i], sems.at[i]) for i in range(count)]
    for copy in copies:
        copy.start()
    for copy in copies:
        copy.wait()
    total = held[0].astype(jnp.float32)
    for i in range(1, count):
        total = total + held[i].astype(jnp.float32)
    refs[-2][...] = total.astype(refs[-2].dtype)
    last = pltpu.make_async_copy(refs[-2], out, sems.at[0])
    last.start()
    last.wait()


def inner_weights(lam, block):
    rows = lam[0].shape[1]
    lane = lax.broadcasted_iota(jnp.int32, (8, rows), 1)
    sub = lax.broadcasted_iota(jnp.int32, (8, rows), 0)
    zero = jnp.zeros((8, rows), jnp.float32)
    near = zero
    differ = (lane & 7) ^ sub
    for level in range(1, 4):
        near = jnp.where((differ >> (level - 1)) == 1, lam[level], near)
    near = jnp.where(differ == 0, lam[0], near)
    near = jnp.where(sub <= (lane & 7), near, zero)
    group = (lane >> 3) & (block // 8 - 1)
    out = []
    for first in range(0, block // 8, 8):
        index = sub + first
        apart = index ^ group
        far = zero
        for level in range(4, block.bit_length()):
            far = jnp.where((apart >> (level - 4)) == 1, lam[level], far)
        far = jnp.where(index < group, far, zero)
        for i in range(8):
            wide = jnp.broadcast_to(far[i : i + 1, :], (8, rows))
            out.append(jnp.where(group == first + i, near, wide))
    return out


def choose_kernel(count, place, *refs):
    out, sem = refs[-2:]
    mine = (place[0] >> 2) & (count - 1)
    for low in range(count):

        @pl.when(mine == low)
        def _(low=low):
            copy = pltpu.make_async_copy(refs[low], out, sem)
            copy.start()
            copy.wait()


def pack_kernel(count, *refs):
    out, sems = refs[-2:]
    copies = [pltpu.make_async_copy(refs[i], out.at[i], sems.at[i]) for i in range(count)]
    for copy in copies:
        copy.start()
    for copy in copies:
        copy.wait()


def inside_kernel(where, place, x, even, odd, w, k_in, vt_in, codes, after, q_out, in_out):
    rows = x.shape[1]
    heads, dim = vt_in.shape[:2]
    base = base_of(place, where, heads)
    block, wide = min(128, rows), min(256, rows)
    bits = rows.bit_length() - 1

    @pl.loop(0, heads // GROUP)
    def _(step):
        for unit in range(GROUP):
            head = step * GROUP + unit
            cols = lanes(head, dim)
            queries = convolve(x, 0, place, even, odd, w, 0, base + head, dim)
            q_out[:, cols] = queries
            lam = [
                codes[level, pl.ds(base + head, 1), :].astype(jnp.float32) * 0.125
                for level in range(bits + 1)
            ]
            near = inner_weights(lam, block)
            for first in range(0, rows, wide):
                reach = first + wide
                scores = lax.dot_general(
                    k_in[0:reach, cols],
                    queries[first:reach],
                    NT,
                    preferred_element_type=jnp.float32,
                )
                columns = []
                for t0 in range(first, reach, block):
                    span = slice(t0 - first, t0 - first + block)
                    parts = []
                    for s0 in range(0, reach, block):
                        if s0 > t0:
                            parts.append(jnp.zeros((block, block), jnp.bfloat16))
                            continue
                        if s0 == t0:
                            weight = jnp.concatenate([n[:, t0 : t0 + block] for n in near], 0)
                        else:
                            weight = lam[(s0 ^ t0).bit_length()][:, t0 : t0 + block]
                        parts.append((scores[s0 : s0 + block, span] * weight).astype(jnp.bfloat16))
                    columns.append(jnp.concatenate(parts, 0))
                in_out[head, :, first:reach] = jnp.dot(
                    vt_in[head, :, 0:reach],
                    jnp.concatenate(columns, 1),
                    preferred_element_type=jnp.float32,
                )


def across_kernel(bits, inner, held, where, slots, place, q_in, in_in, codes, gain, *rest):
    states, out, token = rest[:bits], rest[bits + held], rest[bits + held + 1]
    fen, mixed, sems = rest[bits + held + 2 :]
    token[...] = jnp.zeros_like(token)
    heads, dim, rows = in_in.shape
    base = base_of(place, where, heads)
    copies = [
        pltpu.make_async_copy(
            states[bit] if slots[bit] is None else states[bit].at[slots[bit]],
            fen.at[:, bit * dim : (bit + 1) * dim, :],
            sems.at[bit],
        )
        for bit in range(bits)
    ]
    for copy in copies:
        copy.start()
    for copy in copies:
        copy.wait()
    scales = [((place[0] >> bit) & 1).astype(jnp.float32) * 0.125 for bit in range(bits)]
    wide = min(256, rows)

    @pl.loop(0, heads // GROUP)
    def _(step):
        for unit in range(GROUP):
            head = step * GROUP + unit
            cols = lanes(head, dim)
            lam = [
                codes[inner + bit, pl.ds(base + head, 1), :].astype(jnp.float32) * scales[bit]
                for bit in range(bits)
            ]
            for t0 in range(0, rows, wide):
                span = slice(t0, t0 + wide)
                parts = lax.dot_general(
                    fen[head], q_in[span, cols], NT, preferred_element_type=jnp.float32
                )
                total = in_in[head, :, span]
                for bit in range(bits):
                    total = total + lam[bit][:, span] * parts[bit * dim : (bit + 1) * dim]
                mean = jnp.sum(total * total, 0, keepdims=True) * (1.0 / dim)
                normed = total * lax.rsqrt(mean + 1e-06)
                mixed[span, cols] = (normed.T * gain[:, lanes(base + head, dim)]).astype(
                    jnp.bfloat16
                )

    width = heads * dim
    home = out.at[:, pl.ds(pl.multiple_of(base * dim, width), width)]
    last = pltpu.make_async_copy(mixed, home, sems.at[bits])
    last.start()
    last.wait()


def spread(wanted, count):
    pairs, free = dict(wanted), [i for i in range(count) if i not in wanted.values()]
    for i in range(count):
        if i not in pairs:
            good = [k for k in (i + 1, i - 1) if k in free] + [k for k in free if k != i] + free
            pairs[i] = good[0]
            free.remove(good[0])
    return sorted(pairs.items())


def on_device(projected, conv_weight, level_codes, out_gain):
    taps = conv_weight.shape[1]
    rows, width = projected.shape[1:]
    levels, head_count = level_codes.shape[:2]
    dim = width // head_count
    tok_bits = rows.bit_length() - 1
    count = lax.axis_size("ctx")
    bits = count.bit_length() - 1
    index = lax.axis_index("ctx")
    quarter = head_count // 4
    bf16, f32 = jnp.bfloat16, jnp.float32

    def exchange(value, bit):
        return lax.ppermute(value, "ctx", [(i, i ^ (1 << bit)) for i in range(count)])

    edge = projected[:, rows - taps + 1 :, :]
    steps = {i: i + 1 for i in range(1, count - 2, 2)} | {i: i - 1 for i in range(4, count - 2, 2)}
    steps |= {0: 1, 2: 0, count - 2: count - 1, count - 1: count - 3}
    rim_even = lax.ppermute(edge, "ctx", sorted(steps.items()))
    rim_odd = exchange(edge, 0)

    def kept(value):
        return pltpu.with_memory_space_constraint(value, VMEM)

    place = index.reshape(1).astype(jnp.int32)
    params = pltpu.CompilerParams(vmem_limit_bytes=ROOM)
    whole = pl.BlockSpec(memory_space=VMEM)
    scalars = pl.BlockSpec(memory_space=pltpu.SMEM)
    anywhere = pl.BlockSpec(memory_space=pl.ANY)
    state = jax.ShapeDtypeStruct((quarter, dim, dim), bf16)

    def staged(first, shape, arrays, after):
        shapes = [shape] + [a.shape for a in arrays[1:]]
        homes = [pltpu.with_memory_space_constraint(a, pltpu.HBM) for a in arrays]
        brought = pl.pallas_call(
            functools.partial(stage_kernel, len(homes), first),
            in_specs=[anywhere] * (len(homes) + 1),
            out_specs=[whole] * len(homes),
            out_shape=[VMEM(size, a.dtype) for size, a in zip(shapes, arrays)],
            scratch_shapes=[pltpu.SemaphoreType.DMA((len(homes),))],
            compiler_params=params,
            name="stage",
        )(*homes, after)
        return map(kept, brought)

    def key_value(where, got=None, after=None):
        merge, extra = got is not None, 0 if after is None else 1
        operands = [place, rim_even, rim_odd, weight, source]
        specs = [scalars] + [whole] * 4
        made = [VMEM((rows, quarter * dim), bf16), VMEM((quarter, dim, rows), bf16), state]
        scratch = []
        if merge:
            operands.append(got)
            made.append(state)
            scratch = [VMEM(state.shape, bf16), pltpu.SemaphoreType.DMA((1,))]
        if extra:
            operands.append(after)
        return pl.pallas_call(
            functools.partial(kv_kernel, merge, extra, where),
            in_specs=specs + [anywhere] * (len(operands) - len(specs)),
            out_specs=[whole] * len(made),
            out_shape=made,
            scratch_shapes=scratch,
            compiler_params=params,
            name="key_value",
        )(*operands)

    def merged(values, after):
        return pl.pallas_call(
            merge_kernel,
            in_specs=[anywhere] * (len(values) + len(after)),
            out_specs=anywhere,
            out_shape=state,
            scratch_shapes=[
                VMEM((len(values), *state.shape), bf16),
                VMEM(state.shape, bf16),
                pltpu.SemaphoreType.DMA((len(values),)),
            ],
            compiler_params=params,
            name="merge",
        )(*values, *after)

    def chosen(values, after):
        return pl.pallas_call(
            functools.partial(choose_kernel, len(values)),
            in_specs=[scalars] + [anywhere] * (len(values) + len(after)),
            out_specs=anywhere,
            out_shape=state,
            scratch_shapes=[pltpu.SemaphoreType.DMA],
            compiler_params=params,
            name="choose",
        )(place, *values, *after)

    def packed(values, after):
        shape = (len(values), *state.shape)
        return pl.pallas_call(
            functools.partial(pack_kernel, len(values)),
            in_specs=[anywhere] * (len(values) + len(after)),
            out_specs=anywhere,
            out_shape=jax.ShapeDtypeStruct(shape, bf16),
            scratch_shapes=[pltpu.SemaphoreType.DMA((len(values),))],
            compiler_params=params,
            name="pack",
        )(*values, *after)

    def inside(where, after):
        return pl.pallas_call(
            functools.partial(inside_kernel, where),
            in_specs=[scalars] + [whole] * 7 + [anywhere],
            out_specs=[whole] * 2,
            out_shape=[VMEM((rows, quarter * dim), bf16), VMEM((quarter, dim, rows), f32)],
            compiler_params=params,
            name="inside",
        )(
            place, raw, rim_even, rim_odd, weight, kept(keys[where]), kept(values[where]), codes, after
        )

    def across(where, local, states, out):
        held = [] if out is None else [out]
        queries, inner = local
        states, slots = zip(*(a if isinstance(a, tuple) else (a, None) for a in states))
        return pl.pallas_call(
            functools.partial(across_kernel, bits, tok_bits + 1, len(held), where, slots),
            in_specs=[scalars] + [whole] * 4 + [anywhere] * (bits + len(held)),
            out_specs=[anywhere, whole],
            out_shape=[jax.ShapeDtypeStruct((rows, width), bf16), VMEM((8, 128), f32)],
            input_output_aliases={5 + bits: 0} if held else {},
            scratch_shapes=[
                VMEM((quarter, bits * dim, dim), bf16),
                VMEM((rows, quarter * dim), bf16),
                pltpu.SemaphoreType.DMA((bits + 1,)),
            ],
            compiler_params=params,
            name="across",
        )(place, kept(queries), kept(inner), codes, gain, *states, *held)

    near, far, other_near, other_far = (0, 0), (0, 1), (1, 0), (1, 1)
    keys, values, local = {}, {}, {}
    source, weight = staged(1, (2, rows, width), (projected, conv_weight), edge)
    keys[other_far], values[other_far], sent = key_value(other_far)
    got_far = exchange(sent, 0)
    keys[other_near], values[other_near], sent = key_value(other_near, after=sent)
    got_near = exchange(sent, 0)
    keys[far], values[far], state_far, total_far = key_value(far, got_far, after=sent)
    near1 = exchange(total_far, 1)
    keys[near], values[near], state_near, total_near = key_value(near, got_near, after=total_far)
    far1 = exchange(total_near, 1)
    rest = (projected, level_codes, out_gain.reshape(1, width))
    raw, codes, gain = staged(0, (1, rows, width), rest, total_near)
    nears, fars = [got_near, near1], [got_far, far1]
    waiting = [near, far, other_near, other_far]

    def work(where, after):
        waiting.remove(where)
        local[where] = inside(where, after)
        return local[where][1]

    running = merged([total_near, near1], [work(near, total_near)])
    for bit in range(2, bits):
        ones = (1 << bit) - 4
        if bit == 2:
            pieces = [exchange(running, bit)]
        else:
            pieces = []
            for low in reversed(range(1 << (bit - 2))):
                holders = [
                    i for i in range(count // 4) if i << 2 & ones == ones and not i << 2 >> bit & 1
                ]
                wanted = {i: (i & ~(ones >> 2)) | low | (1 << (bit - 2)) for i in holders}
                pairs = [(i * 4 + j, k * 4 + j) for i, k in spread(wanted, count // 4) for j in range(4)]
                pieces.append(lax.ppermute(running, "ctx", pairs))
        after = []
        for _ in range(bit - 1):
            if waiting:
                after.append(work(waiting[0], after[-1] if after else running))
        got = chosen(pieces[::-1], after) if len(pieces) > 1 else pieces[0]
        if bit + 1 < bits:
            running = merged([running, got], after)
        nears.append(got)
        fars.append(exchange(got, 1))
        if bit == 2:
            early = exchange(packed([state_near, near1, state_far, far1], [running]), 0)
    late = exchange(packed(nears[2:] + fars[2:-1], []), 0)
    later = bits - 2
    other_nears = [(early, 0), (early, 1)] + [(late, i) for i in range(later)]
    after = [work(where, nears[-1]) for where in list(waiting)]
    out, token = across(near, local[near], nears, None)
    out, token = across(other_near, local[other_near], other_nears, out)
    last = merged(fars[-1:], after + [token])
    other_fars = [(early, 2), (early, 3)] + [(late, later + i) for i in range(later - 1)]
    other_fars.append(exchange(last, 0))
    out, _ = across(far, local[far], fars[:-1] + [last], out)
    return across(other_far, local[other_far], other_fars, out)[0]


def solution(mesh):
    placed = (P(None, ("groups", "ctx"), None), P(), P(None, None, ("groups", "ctx")), P())
    return jax.shard_map(
        on_device, mesh=mesh, in_specs=placed, out_specs=P(("groups", "ctx"), None), check_vma=False
    )
```

```python
import functools

import jax
import jax.numpy as jnp
from jax import lax
from jax.experimental import pallas as pl
from jax.experimental.pallas import tpu as pltpu
from jax.sharding import PartitionSpec as P

NT = (((1,), (1,)), ((), ()))
ROOM = 8 * 1024 * 1024
GROUP = 8
CHUNK = 4
VMEM = pltpu.VMEM


def lanes(head, dim):
    return pl.ds(pl.multiple_of(head * dim, dim), dim)


def base_of(place, where, heads):
    index = place[0]
    return (((index & 1) ^ where[0]) * 2 + (((index >> 1) & 1) ^ where[1])) * heads


def before_span(place, even, odd, which, cols):
    index = place[0]
    rows = jnp.where((index & 1) == 1, odd[which, :, cols], even[which, :, cols])
    return jnp.where(index == 0, 0.0, rows.astype(jnp.float32))


def convolve(x, at, place, even, odd, w, which, head, dim, step=128):
    rows, taps = x.shape[1], w.shape[1]
    cols = lanes(head, dim)
    w_rows = [w[which, tap : tap + 1, cols] for tap in range(taps)]
    before = jnp.concatenate(
        [jnp.zeros((9 - taps, dim), jnp.float32), before_span(place, even, odd, which, cols)], 0
    )
    out = []
    for row in range(0, rows, step):
        chunk = x[at, row : row + step, cols].astype(jnp.float32)
        full = jnp.concatenate([before, chunk], 0)
        total = None
        for tap in range(taps - 2, -1, -2):
            pair = w_rows[tap + 1] * full + w_rows[tap] * pltpu.roll(full, 1, 0)
            if tap < taps - 2:
                pair = pltpu.roll(pair, taps - 2 - tap, 0)
            total = pair if total is None else total + pair
        out.append(total[8:].astype(jnp.bfloat16))
        before = chunk[step - 8 :]
    return jnp.concatenate(out, 0)


def stage_kernel(count, first, *refs):
    outs, sems = refs[-1 - count : -1], refs[-1]
    copies = [
        pltpu.make_async_copy(home, out, sems.at[i])
        for i, (home, out) in enumerate(zip(refs, outs))
        if home.shape == out.shape
    ]
    if refs[0].shape != outs[0].shape:
        part = refs[0].at[first : first + outs[0].shape[0]]
        copies.append(pltpu.make_async_copy(part, outs[0], sems.at[0]))
    for copy in copies:
        copy.start()
    for copy in copies:
        copy.wait()


def kv_kernel(merge, extra, where, place, even, odd, w, x, *rest):
    if merge:
        got_home, rest, got, sems = rest[0], rest[1:-2], rest[-2], rest[-1]
        copy = pltpu.make_async_copy(got_home, got, sems.at[0])
        copy.start()
    rest = rest[extra:]
    k_out, vt_out, s_out = rest[:3]
    heads, dim = vt_out.shape[:2]
    base = base_of(place, where, heads)
    if merge:
        sum_out = rest[3]
        copy.wait()

    @pl.loop(0, heads // GROUP)
    def _(step):
        for unit in range(GROUP):
            head = step * GROUP + unit
            keys = convolve(x, 0, place, even, odd, w, 1, base + head, dim)
            k_out[:, lanes(head, dim)] = keys
            vt = convolve(x, 1, place, even, odd, w, 2, base + head, dim).T
            vt_out[head] = vt
            state = jnp.dot(vt, keys, preferred_element_type=jnp.float32)
            s_out[head] = state.astype(jnp.bfloat16)
            if merge:
                sum_out[head] = (state + got[head].astype(jnp.float32)).astype(jnp.bfloat16)


def merge_kernel(*refs):
    count = refs[-1].shape[0]
    out, held, sems = refs[-4], refs[-3], refs[-1]
    copies = [pltpu.make_async_copy(refs[i], held.at[i], sems.at[i]) for i in range(count)]
    for copy in copies:
        copy.start()
    for copy in copies:
        copy.wait()
    total = held[0].astype(jnp.float32)
    for i in range(1, count):
        total = total + held[i].astype(jnp.float32)
    refs[-2][...] = total.astype(refs[-2].dtype)
    last = pltpu.make_async_copy(refs[-2], out, sems.at[0])
    last.start()
    last.wait()


def inner_weights(lam, block):
    rows = lam[0].shape[1]
    lane = lax.broadcasted_iota(jnp.int32, (8, rows), 1)
    sub = lax.broadcasted_iota(jnp.int32, (8, rows), 0)
    zero = jnp.zeros((8, rows), jnp.float32)
    near = zero
    differ = (lane & 7) ^ sub
    for level in range(1, 4):
        near = jnp.where((differ >> (level - 1)) == 1, lam[level], near)
    near = jnp.where(differ == 0, lam[0], near)
    near = jnp.where(sub <= (lane & 7), near, zero)
    group = (lane >> 3) & (block // 8 - 1)
    out = []
    for first in range(0, block // 8, 8):
        index = sub + first
        apart = index ^ group
        far = zero
        for level in range(4, block.bit_length()):
            far = jnp.where((apart >> (level - 4)) == 1, lam[level], far)
        far = jnp.where(index < group, far, zero)
        for i in range(8):
            wide = jnp.broadcast_to(far[i : i + 1, :], (8, rows))
            out.append(jnp.where(group == first + i, near, wide))
    return out


def choose_kernel(count, place, *refs):
    out, sem = refs[-2:]
    mine = (place[0] >> 2) & (count - 1)
    for low in range(count):

        @pl.when(mine == low)
        def _(low=low):
            copy = pltpu.make_async_copy(refs[low], out, sem)
            copy.start()
            copy.wait()


def pack_kernel(count, *refs):
    out, sems = refs[-2:]
    copies = [pltpu.make_async_copy(refs[i], out.at[i], sems.at[i]) for i in range(count)]
    for copy in copies:
        copy.start()
    for copy in copies:
        copy.wait()


def inside_kernel(where, place, x, even, odd, w, k_in, vt_in, codes, after, q_out, in_out):
    rows = x.shape[1]
    heads, dim = vt_in.shape[:2]
    base = base_of(place, where, heads)
    block, wide = min(128, rows), min(256, rows)
    bits = rows.bit_length() - 1

    @pl.loop(0, heads // GROUP)
    def _(step):
        for unit in range(GROUP):
            head = step * GROUP + unit
            cols = lanes(head, dim)
            queries = convolve(x, 0, place, even, odd, w, 0, base + head, dim)
            q_out[:, cols] = queries
            lam = [
                codes[level, pl.ds(base + head, 1), :].astype(jnp.float32) * 0.125
                for level in range(bits + 1)
            ]
            near = inner_weights(lam, block)
            for first in range(0, rows, wide):
                reach = first + wide
                scores = lax.dot_general(
                    k_in[0:reach, cols],
                    queries[first:reach],
                    NT,
                    preferred_element_type=jnp.float32,
                )
                columns = []
                for t0 in range(first, reach, block):
                    span = slice(t0 - first, t0 - first + block)
                    parts = []
                    for s0 in range(0, reach, block):
                        if s0 > t0:
                            parts.append(jnp.zeros((block, block), jnp.bfloat16))
                            continue
                        if s0 == t0:
                            weight = jnp.concatenate([n[:, t0 : t0 + block] for n in near], 0)
                        else:
                            weight = lam[(s0 ^ t0).bit_length()][:, t0 : t0 + block]
                        parts.append((scores[s0 : s0 + block, span] * weight).astype(jnp.bfloat16))
                    columns.append(jnp.concatenate(parts, 0))
                in_out[head, :, first:reach] = jnp.dot(
                    vt_in[head, :, 0:reach],
                    jnp.concatenate(columns, 1),
                    preferred_element_type=jnp.float32,
                )


def across_kernel(bits, inner, held, where, slots, place, q_in, in_in, codes, gain, *rest):
    states, out, token = rest[:bits], rest[bits + held], rest[bits + held + 1]
    mixed, sems = rest[bits + held + 2 :]
    token[...] = jnp.zeros_like(token)
    heads, dim, rows = in_in.shape
    base = base_of(place, where, heads)
    width = CHUNK * dim

    def ship(chunk):
        source = mixed.at[:, pl.ds(pl.multiple_of(chunk * width, width), width)]
        home = out.at[:, pl.ds(pl.multiple_of(base * dim + chunk * width, width), width)]
        return pltpu.make_async_copy(source, home, sems.at[chunk])

    scales = [((place[0] >> bit) & 1).astype(jnp.float32) * 0.125 for bit in range(bits)]
    wide = min(256, rows)

    @pl.loop(0, heads // GROUP)
    def _(step):
        for unit in range(GROUP):
            head = step * GROUP + unit
            cols = lanes(head, dim)
            lam = [
                codes[inner + bit, pl.ds(base + head, 1), :].astype(jnp.float32) * scales[bit]
                for bit in range(bits)
            ]
            fenwick = jnp.concatenate(
                [
                    state[head] if slot is None else state[slot, head]
                    for state, slot in zip(states, slots)
                ],
                0,
            )
            for t0 in range(0, rows, wide):
                span = slice(t0, t0 + wide)
                parts = lax.dot_general(
                    fenwick, q_in[span, cols], NT, preferred_element_type=jnp.float32
                )
                total = in_in[head, :, span]
                for bit in range(bits):
                    total = total + lam[bit][:, span] * parts[bit * dim : (bit + 1) * dim]
                mean = jnp.sum(total * total, 0, keepdims=True) * (1.0 / dim)
                normed = total * lax.rsqrt(mean + 1e-06)
                mixed[span, cols] = (normed.T * gain[:, lanes(base + head, dim)]).astype(
                    jnp.bfloat16
                )

            if (unit + 1) % CHUNK == 0:
                ship(step * (GROUP // CHUNK) + unit // CHUNK).start()

    for chunk in range(heads // CHUNK):
        ship(chunk).wait()


def spread(wanted, count):
    pairs, free = dict(wanted), [i for i in range(count) if i not in wanted.values()]
    for i in range(count):
        if i not in pairs:
            good = [k for k in (i + 1, i - 1) if k in free] + [k for k in free if k != i] + free
            pairs[i] = good[0]
            free.remove(good[0])
    return sorted(pairs.items())


def on_device(projected, conv_weight, level_codes, out_gain):
    taps = conv_weight.shape[1]
    rows, width = projected.shape[1:]
    levels, head_count = level_codes.shape[:2]
    dim = width // head_count
    tok_bits = rows.bit_length() - 1
    count = lax.axis_size("ctx")
    bits = count.bit_length() - 1
    index = lax.axis_index("ctx")
    quarter = head_count // 4
    bf16, f32 = jnp.bfloat16, jnp.float32

    def exchange(value, bit):
        return lax.ppermute(value, "ctx", [(i, i ^ (1 << bit)) for i in range(count)])

    edge = projected[:, rows - taps + 1 :, :]
    steps = {i: i + 1 for i in range(1, count - 2, 2)} | {i: i - 1 for i in range(4, count - 2, 2)}
    steps |= {0: 1, 2: 0, count - 2: count - 1, count - 1: count - 3}
    rim_even = lax.ppermute(edge, "ctx", sorted(steps.items()))
    rim_odd = exchange(edge, 0)

    def kept(value):
        return pltpu.with_memory_space_constraint(value, VMEM)

    place = index.reshape(1).astype(jnp.int32)
    params = pltpu.CompilerParams(vmem_limit_bytes=ROOM)
    whole = pl.BlockSpec(memory_space=VMEM)
    scalars = pl.BlockSpec(memory_space=pltpu.SMEM)
    anywhere = pl.BlockSpec(memory_space=pl.ANY)
    state = jax.ShapeDtypeStruct((quarter, dim, dim), bf16)

    def staged(first, shape, arrays, after):
        shapes = [shape] + [a.shape for a in arrays[1:]]
        homes = [pltpu.with_memory_space_constraint(a, pltpu.HBM) for a in arrays]
        brought = pl.pallas_call(
            functools.partial(stage_kernel, len(homes), first),
            in_specs=[anywhere] * (len(homes) + 1),
            out_specs=[whole] * len(homes),
            out_shape=[VMEM(size, a.dtype) for size, a in zip(shapes, arrays)],
            scratch_shapes=[pltpu.SemaphoreType.DMA((len(homes),))],
            compiler_params=params,
            name="stage",
        )(*homes, after)
        return map(kept, brought)

    def key_value(where, got=None, after=None):
        merge, extra = got is not None, 0 if after is None else 1
        operands = [place, rim_even, rim_odd, weight, source]
        specs = [scalars] + [whole] * 4
        made = [VMEM((rows, quarter * dim), bf16), VMEM((quarter, dim, rows), bf16), state]
        scratch = []
        if merge:
            operands.append(got)
            made.append(state)
            scratch = [VMEM(state.shape, bf16), pltpu.SemaphoreType.DMA((1,))]
        if extra:
            operands.append(after)
        return pl.pallas_call(
            functools.partial(kv_kernel, merge, extra, where),
            in_specs=specs + [anywhere] * (len(operands) - len(specs)),
            out_specs=[whole] * len(made),
            out_shape=made,
            scratch_shapes=scratch,
            compiler_params=params,
            name="key_value",
        )(*operands)

    def merged(values, after):
        return pl.pallas_call(
            merge_kernel,
            in_specs=[anywhere] * (len(values) + len(after)),
            out_specs=anywhere,
            out_shape=state,
            scratch_shapes=[
                VMEM((len(values), *state.shape), bf16),
                VMEM(state.shape, bf16),
                pltpu.SemaphoreType.DMA((len(values),)),
            ],
            compiler_params=params,
            name="merge",
        )(*values, *after)

    def chosen(values, after):
        return pl.pallas_call(
            functools.partial(choose_kernel, len(values)),
            in_specs=[scalars] + [anywhere] * (len(values) + len(after)),
            out_specs=anywhere,
            out_shape=state,
            scratch_shapes=[pltpu.SemaphoreType.DMA],
            compiler_params=params,
            name="choose",
        )(place, *values, *after)

    def packed(values, after):
        shape = (len(values), *state.shape)
        return pl.pallas_call(
            functools.partial(pack_kernel, len(values)),
            in_specs=[anywhere] * (len(values) + len(after)),
            out_specs=anywhere,
            out_shape=jax.ShapeDtypeStruct(shape, bf16),
            scratch_shapes=[pltpu.SemaphoreType.DMA((len(values),))],
            compiler_params=params,
            name="pack",
        )(*values, *after)

    def inside(where, after):
        return pl.pallas_call(
            functools.partial(inside_kernel, where),
            in_specs=[scalars] + [whole] * 7 + [anywhere],
            out_specs=[whole] * 2,
            out_shape=[VMEM((rows, quarter * dim), bf16), VMEM((quarter, dim, rows), f32)],
            compiler_params=params,
            name="inside",
        )(
            place, raw, rim_even, rim_odd, weight, kept(keys[where]), kept(values[where]), codes, after
        )

    def across(where, local, states, out):
        held = [] if out is None else [out]
        queries, inner = local
        states, slots = zip(*(a if isinstance(a, tuple) else (a, None) for a in states))
        return pl.pallas_call(
            functools.partial(across_kernel, bits, tok_bits + 1, len(held), where, slots),
            in_specs=[scalars] + [whole] * (4 + bits) + [anywhere] * len(held),
            out_specs=[anywhere, whole],
            out_shape=[jax.ShapeDtypeStruct((rows, width), bf16), VMEM((8, 128), f32)],
            input_output_aliases={5 + bits: 0} if held else {},
            scratch_shapes=[
                VMEM((rows, quarter * dim), bf16),
                pltpu.SemaphoreType.DMA((quarter // CHUNK,)),
            ],
            compiler_params=params,
            name="across",
        )(place, kept(queries), kept(inner), codes, gain, *map(kept, states), *held)

    near, far, other_near, other_far = (0, 0), (0, 1), (1, 0), (1, 1)
    keys, values, local = {}, {}, {}
    source, weight = staged(1, (2, rows, width), (projected, conv_weight), edge)
    keys[other_far], values[other_far], sent = key_value(other_far)
    got_far = exchange(sent, 0)
    keys[other_near], values[other_near], sent = key_value(other_near, after=sent)
    got_near = exchange(sent, 0)
    keys[far], values[far], state_far, total_far = key_value(far, got_far, after=sent)
    near1 = exchange(total_far, 1)
    keys[near], values[near], state_near, total_near = key_value(near, got_near, after=total_far)
    far1 = exchange(total_near, 1)
    rest = (projected, level_codes, out_gain.reshape(1, width))
    raw, codes, gain = staged(0, (1, rows, width), rest, total_near)
    nears, fars = [got_near, near1], [got_far, far1]
    waiting = [near, far, other_near, other_far]

    def work(where, after):
        waiting.remove(where)
        local[where] = inside(where, after)
        return local[where][1]

    early = exchange(packed([state_near, state_far], [total_near]), 0)
    running = merged([total_near, near1], [raw])
    for bit in range(2, bits):
        ones = (1 << bit) - 4
        if bit == 2:
            pieces = [exchange(running, bit)]
        else:
            pieces = []
            for low in reversed(range(1 << (bit - 2))):
                holders = [
                    i for i in range(count // 4) if i << 2 & ones == ones and not i << 2 >> bit & 1
                ]
                wanted = {i: (i & ~(ones >> 2)) | low | (1 << (bit - 2)) for i in holders}
                pairs = [(i * 4 + j, k * 4 + j) for i, k in spread(wanted, count // 4) for j in range(4)]
                pieces.append(lax.ppermute(running, "ctx", pairs))
        after = []
        for _ in range(2):
            if waiting:
                after.append(work(waiting[0], after[-1] if after else running))
        got = chosen(pieces[::-1], after) if len(pieces) > 1 else pieces[0]
        if bit + 1 < bits:
            running = merged([running, got], after + [early, far1])
        nears.append(got)
        fars.append(exchange(got, 1))
    late = exchange(packed(nears[1:] + fars[1:-1], []), 0)
    later = bits - 1
    other_nears = [(early, 0)] + [(late, i) for i in range(later)]
    after = [work(where, nears[-1]) for where in list(waiting)]
    out, token = across(near, local[near], nears, None)
    out, token = across(other_near, local[other_near], other_nears, out)
    last = merged(fars[-1:], after + [token])
    other_fars = [(early, 1)] + [(late, later + i) for i in range(later - 1)]
    other_fars.append(exchange(last, 0))
    out, _ = across(far, local[far], fars[:-1] + [last], out)
    return across(other_far, local[other_far], other_fars, out)[0]


def solution(mesh):
    placed = (P(None, ("groups", "ctx"), None), P(), P(None, None, ("groups", "ctx")), P())
    return jax.shard_map(
        on_device, mesh=mesh, in_specs=placed, out_specs=P(("groups", "ctx"), None), check_vma=False
    )
```

```python
import functools

import jax
import jax.numpy as jnp
from jax import lax
from jax.experimental import pallas as pl
from jax.experimental.pallas import tpu as pltpu
from jax.sharding import PartitionSpec as P

NT = (((1,), (1,)), ((), ()))
ROOM = 8 * 1024 * 1024
GROUP = 8
WIDE = 8
CHUNK = 2
VMEM = pltpu.VMEM


def lanes(head, dim):
    return pl.ds(pl.multiple_of(head * dim, dim), dim)


def base_of(place, where, heads):
    index = place[0]
    return (((index & 1) ^ where[0]) * 2 + (((index >> 1) & 1) ^ where[1])) * heads


def before_span(place, even, odd, which, cols):
    index = place[0]
    rows = jnp.where((index & 1) == 1, odd[which, :, cols], even[which, :, cols])
    return jnp.where(index == 0, 0.0, rows.astype(jnp.float32))


def convolve(x, at, place, even, odd, w, which, head, dim, step=128):
    rows, taps = x.shape[1], w.shape[1]
    cols = lanes(head, dim)
    w_rows = [w[which, tap : tap + 1, cols] for tap in range(taps)]
    before = jnp.concatenate(
        [jnp.zeros((9 - taps, dim), jnp.float32), before_span(place, even, odd, which, cols)], 0
    )
    out = []
    for row in range(0, rows, step):
        chunk = x[at, row : row + step, cols].astype(jnp.float32)
        full = jnp.concatenate([before, chunk], 0)
        total = None
        for tap in range(taps - 2, -1, -2):
            pair = w_rows[tap + 1] * full + w_rows[tap] * pltpu.roll(full, 1, 0)
            if tap < taps - 2:
                pair = pltpu.roll(pair, taps - 2 - tap, 0)
            total = pair if total is None else total + pair
        out.append(total[8:].astype(jnp.bfloat16))
        before = chunk[step - 8 :]
    return jnp.concatenate(out, 0)


def stage_kernel(count, first, *refs):
    outs, sems = refs[-1 - count : -1], refs[-1]
    copies = [
        pltpu.make_async_copy(home, out, sems.at[i])
        for i, (home, out) in enumerate(zip(refs, outs))
        if home.shape == out.shape
    ]
    if refs[0].shape != outs[0].shape:
        part = refs[0].at[first : first + outs[0].shape[0]]
        copies.append(pltpu.make_async_copy(part, outs[0], sems.at[0]))
    for copy in copies:
        copy.start()
    for copy in copies:
        copy.wait()


def kv_kernel(merge, extra, where, place, even, odd, w, x, *rest):
    if merge:
        got_home, rest, got, sems = rest[0], rest[1:-2], rest[-2], rest[-1]
        copy = pltpu.make_async_copy(got_home, got, sems.at[0])
        copy.start()
    rest = rest[extra:]
    k_out, vt_out, s_out = rest[:3]
    heads, dim = vt_out.shape[:2]
    base = base_of(place, where, heads)
    if merge:
        sum_out = rest[3]
        copy.wait()

    @pl.loop(0, heads // GROUP)
    def _(step):
        for unit in range(GROUP):
            head = step * GROUP + unit
            keys = convolve(x, 0, place, even, odd, w, 1, base + head, dim)
            k_out[:, lanes(head, dim)] = keys
            vt = convolve(x, 1, place, even, odd, w, 2, base + head, dim).T
            vt_out[head] = vt
            state = jnp.dot(vt, keys, preferred_element_type=jnp.float32)
            s_out[head] = state.astype(jnp.bfloat16)
            if merge:
                sum_out[head] = (state + got[head].astype(jnp.float32)).astype(jnp.bfloat16)


def merge_kernel(*refs):
    count = refs[-1].shape[0]
    out, held, sems = refs[-4], refs[-3], refs[-1]
    copies = [pltpu.make_async_copy(refs[i], held.at[i], sems.at[i]) for i in range(count)]
    for copy in copies:
        copy.start()
    for copy in copies:
        copy.wait()
    total = held[0].astype(jnp.float32)
    for i in range(1, count):
        total = total + held[i].astype(jnp.float32)
    refs[-2][...] = total.astype(refs[-2].dtype)
    last = pltpu.make_async_copy(refs[-2], out, sems.at[0])
    last.start()
    last.wait()


def inner_weights(lam, block):
    rows = lam[0].shape[1]
    lane = lax.broadcasted_iota(jnp.int32, (8, rows), 1)
    sub = lax.broadcasted_iota(jnp.int32, (8, rows), 0)
    zero = jnp.zeros((8, rows), jnp.float32)
    near = zero
    differ = (lane & 7) ^ sub
    for level in range(1, 4):
        near = jnp.where((differ >> (level - 1)) == 1, lam[level], near)
    near = jnp.where(differ == 0, lam[0], near)
    near = jnp.where(sub <= (lane & 7), near, zero)
    group = (lane >> 3) & (block // 8 - 1)
    out = []
    for first in range(0, block // 8, 8):
        index = sub + first
        apart = index ^ group
        far = zero
        for level in range(4, block.bit_length()):
            far = jnp.where((apart >> (level - 4)) == 1, lam[level], far)
        far = jnp.where(index < group, far, zero)
        for i in range(8):
            wide = jnp.broadcast_to(far[i : i + 1, :], (8, rows))
            out.append(jnp.where(group == first + i, near, wide))
    return out


def choose_kernel(count, place, *refs):
    out, sem = refs[-2:]
    mine = (place[0] >> 2) & (count - 1)
    for low in range(count):

        @pl.when(mine == low)
        def _(low=low):
            copy = pltpu.make_async_copy(refs[low], out, sem)
            copy.start()
            copy.wait()


def pack_kernel(count, *refs):
    out, sems = refs[-2:]
    copies = [pltpu.make_async_copy(refs[i], out.at[i], sems.at[i]) for i in range(count)]
    for copy in copies:
        copy.start()
    for copy in copies:
        copy.wait()


def inside_kernel(where, place, x, even, odd, w, k_in, vt_in, codes, after, q_out, in_out):
    rows = x.shape[1]
    heads, dim = vt_in.shape[:2]
    base = base_of(place, where, heads)
    block, wide = min(128, rows), min(256, rows)
    bits = rows.bit_length() - 1

    @pl.loop(0, heads // GROUP)
    def _(step):
        for unit in range(GROUP):
            head = step * GROUP + unit
            cols = lanes(head, dim)
            queries = convolve(x, 0, place, even, odd, w, 0, base + head, dim)
            q_out[:, cols] = queries
            lam = [
                codes[level, pl.ds(base + head, 1), :].astype(jnp.float32) * 0.125
                for level in range(bits + 1)
            ]
            near = inner_weights(lam, block)
            for first in range(0, rows, wide):
                reach = first + wide
                scores = lax.dot_general(
                    k_in[0:reach, cols],
                    queries[first:reach],
                    NT,
                    preferred_element_type=jnp.float32,
                )
                columns = []
                for t0 in range(first, reach, block):
                    span = slice(t0 - first, t0 - first + block)
                    parts = []
                    for s0 in range(0, reach, block):
                        if s0 > t0:
                            parts.append(jnp.zeros((block, block), jnp.bfloat16))
                            continue
                        if s0 == t0:
                            weight = jnp.concatenate([n[:, t0 : t0 + block] for n in near], 0)
                        else:
                            weight = lam[(s0 ^ t0).bit_length()][:, t0 : t0 + block]
                        parts.append((scores[s0 : s0 + block, span] * weight).astype(jnp.bfloat16))
                    columns.append(jnp.concatenate(parts, 0))
                in_out[head, :, first:reach] = jnp.dot(
                    vt_in[head, :, 0:reach],
                    jnp.concatenate(columns, 1),
                    preferred_element_type=jnp.float32,
                )


def across_kernel(bits, inner, held, where, slots, place, q_in, in_in, codes, gain, *rest):
    states, out, token = rest[:bits], rest[bits + held], rest[bits + held + 1]
    mixed, sems = rest[bits + held + 2 :]
    token[...] = jnp.zeros_like(token)
    heads, dim, rows = in_in.shape
    base = base_of(place, where, heads)
    width = CHUNK * dim

    def ship(chunk):
        source = mixed.at[:, pl.ds(pl.multiple_of(chunk * width, width), width)]
        home = out.at[:, pl.ds(pl.multiple_of(base * dim + chunk * width, width), width)]
        return pltpu.make_async_copy(source, home, sems.at[chunk])

    scales = [((place[0] >> bit) & 1).astype(jnp.float32) * 0.125 for bit in range(bits)]
    wide = min(256, rows)

    def work(used):
        @pl.loop(0, heads // WIDE)
        def _(step):
            for unit in range(WIDE):
                head = step * WIDE + unit
                cols = lanes(head, dim)
                lam = [
                    codes[inner + bit, pl.ds(base + head, 1), :].astype(jnp.float32) * scales[bit]
                    for bit in range(used)
                ]
                fenwick = jnp.concatenate(
                    [
                        state[head] if slot is None else state[slot, head]
                        for state, slot in zip(states[:used], slots)
                    ],
                    0,
                )
                for t0 in range(0, rows, wide):
                    span = slice(t0, t0 + wide)
                    parts = lax.dot_general(
                        fenwick, q_in[span, cols], NT, preferred_element_type=jnp.float32
                    )
                    total = in_in[head, :, span]
                    for bit in range(used):
                        total = total + lam[bit][:, span] * parts[bit * dim : (bit + 1) * dim]
                    mean = jnp.sum(total * total, 0, keepdims=True) * (1.0 / dim)
                    normed = total * lax.rsqrt(mean + 1e-06)
                    mixed[span, cols] = (normed.T * gain[:, lanes(base + head, dim)]).astype(
                        jnp.bfloat16
                    )

                if (unit + 1) % CHUNK == 0:
                    ship(step * (WIDE // CHUNK) + unit // CHUNK).start()

    few = min(2, bits)
    pl.when(place[0] < 1 << few)(functools.partial(work, few))
    pl.when(place[0] >= 1 << few)(functools.partial(work, bits))

    for chunk in range(heads // CHUNK):
        ship(chunk).wait()


def spread(wanted, count):
    pairs, free = dict(wanted), [i for i in range(count) if i not in wanted.values()]
    for i in range(count):
        if i not in pairs:
            good = [k for k in (i + 1, i - 1) if k in free] + [k for k in free if k != i] + free
            pairs[i] = good[0]
            free.remove(good[0])
    return sorted(pairs.items())


def on_device(projected, conv_weight, level_codes, out_gain):
    taps = conv_weight.shape[1]
    rows, width = projected.shape[1:]
    levels, head_count = level_codes.shape[:2]
    dim = width // head_count
    tok_bits = rows.bit_length() - 1
    count = lax.axis_size("ctx")
    bits = count.bit_length() - 1
    index = lax.axis_index("ctx")
    quarter = head_count // 4
    bf16, f32 = jnp.bfloat16, jnp.float32

    def exchange(value, bit):
        return lax.ppermute(value, "ctx", [(i, i ^ (1 << bit)) for i in range(count)])

    edge = projected[:, rows - taps + 1 :, :]
    steps = {i: i + 1 for i in range(1, count - 2, 2)} | {i: i - 1 for i in range(4, count - 2, 2)}
    steps |= {0: 1, 2: 0, count - 2: count - 1, count - 1: count - 3}
    rim_even = lax.ppermute(edge, "ctx", sorted(steps.items()))
    rim_odd = exchange(edge, 0)

    def kept(value):
        return pltpu.with_memory_space_constraint(value, VMEM)

    place = index.reshape(1).astype(jnp.int32)
    params = pltpu.CompilerParams(vmem_limit_bytes=ROOM)
    whole = pl.BlockSpec(memory_space=VMEM)
    scalars = pl.BlockSpec(memory_space=pltpu.SMEM)
    anywhere = pl.BlockSpec(memory_space=pl.ANY)
    state = jax.ShapeDtypeStruct((quarter, dim, dim), bf16)

    def staged(first, shape, arrays, after):
        shapes = [shape] + [a.shape for a in arrays[1:]]
        homes = [pltpu.with_memory_space_constraint(a, pltpu.HBM) for a in arrays]
        brought = pl.pallas_call(
            functools.partial(stage_kernel, len(homes), first),
            in_specs=[anywhere] * (len(homes) + 1),
            out_specs=[whole] * len(homes),
            out_shape=[VMEM(size, a.dtype) for size, a in zip(shapes, arrays)],
            scratch_shapes=[pltpu.SemaphoreType.DMA((len(homes),))],
            compiler_params=params,
            name="stage",
        )(*homes, after)
        return map(kept, brought)

    def key_value(where, got=None, after=None):
        merge, extra = got is not None, 0 if after is None else 1
        operands = [place, rim_even, rim_odd, weight, source]
        specs = [scalars] + [whole] * 4
        made = [VMEM((rows, quarter * dim), bf16), VMEM((quarter, dim, rows), bf16), state]
        scratch = []
        if merge:
            operands.append(got)
            made.append(state)
            scratch = [VMEM(state.shape, bf16), pltpu.SemaphoreType.DMA((1,))]
        if extra:
            operands.append(after)
        return pl.pallas_call(
            functools.partial(kv_kernel, merge, extra, where),
            in_specs=specs + [anywhere] * (len(operands) - len(specs)),
            out_specs=[whole] * len(made),
            out_shape=made,
            scratch_shapes=scratch,
            compiler_params=params,
            name="key_value",
        )(*operands)

    def merged(values, after):
        return pl.pallas_call(
            merge_kernel,
            in_specs=[anywhere] * (len(values) + len(after)),
            out_specs=anywhere,
            out_shape=state,
            scratch_shapes=[
                VMEM((len(values), *state.shape), bf16),
                VMEM(state.shape, bf16),
                pltpu.SemaphoreType.DMA((len(values),)),
            ],
            compiler_params=params,
            name="merge",
        )(*values, *after)

    def chosen(values, after):
        return pl.pallas_call(
            functools.partial(choose_kernel, len(values)),
            in_specs=[scalars] + [anywhere] * (len(values) + len(after)),
            out_specs=anywhere,
            out_shape=state,
            scratch_shapes=[pltpu.SemaphoreType.DMA],
            compiler_params=params,
            name="choose",
        )(place, *values, *after)

    def packed(values, after):
        shape = (len(values), *state.shape)
        return pl.pallas_call(
            functools.partial(pack_kernel, len(values)),
            in_specs=[anywhere] * (len(values) + len(after)),
            out_specs=anywhere,
            out_shape=jax.ShapeDtypeStruct(shape, bf16),
            scratch_shapes=[pltpu.SemaphoreType.DMA((len(values),))],
            compiler_params=params,
            name="pack",
        )(*values, *after)

    def inside(where, after):
        return pl.pallas_call(
            functools.partial(inside_kernel, where),
            in_specs=[scalars] + [whole] * 7 + [anywhere],
            out_specs=[whole] * 2,
            out_shape=[VMEM((rows, quarter * dim), bf16), VMEM((quarter, dim, rows), f32)],
            compiler_params=params,
            name="inside",
        )(
            place, raw, rim_even, rim_odd, weight, kept(keys[where]), kept(values[where]), codes, after
        )

    def across(where, local, states, out):
        held = [] if out is None else [out]
        queries, inner = local
        states, slots = zip(*(a if isinstance(a, tuple) else (a, None) for a in states))
        return pl.pallas_call(
            functools.partial(across_kernel, bits, tok_bits + 1, len(held), where, slots),
            in_specs=[scalars] + [whole] * (4 + bits) + [anywhere] * len(held),
            out_specs=[anywhere, whole],
            out_shape=[jax.ShapeDtypeStruct((rows, width), bf16), VMEM((8, 128), f32)],
            input_output_aliases={5 + bits: 0} if held else {},
            scratch_shapes=[
                VMEM((rows, quarter * dim), bf16),
                pltpu.SemaphoreType.DMA((quarter // CHUNK,)),
            ],
            compiler_params=params,
            name="across",
        )(place, kept(queries), kept(inner), codes, gain, *map(kept, states), *held)

    near, far, other_near, other_far = (0, 0), (0, 1), (1, 0), (1, 1)
    keys, values, local = {}, {}, {}
    source, weight = staged(1, (2, rows, width), (projected, conv_weight), edge)
    keys[other_far], values[other_far], sent = key_value(other_far)
    got_far = exchange(sent, 0)
    keys[other_near], values[other_near], sent = key_value(other_near, after=sent)
    got_near = exchange(sent, 0)
    keys[far], values[far], state_far, total_far = key_value(far, got_far, after=sent)
    near1 = exchange(total_far, 1)
    keys[near], values[near], state_near, total_near = key_value(near, got_near, after=total_far)
    far1 = exchange(total_near, 1)
    rest = (projected, level_codes, out_gain.reshape(1, width))
    raw, codes, gain = staged(0, (1, rows, width), rest, total_near)
    nears, fars = [got_near, near1], [got_far, far1]
    waiting = [near, far, other_near, other_far]

    def work(where, after):
        waiting.remove(where)
        local[where] = inside(where, after)
        return local[where][1]

    early = exchange(packed([state_near, state_far], [total_near]), 0)
    running = merged([total_near, near1], [raw])
    for bit in range(2, bits):
        ones = (1 << bit) - 4
        if bit == 2:
            pieces = [exchange(running, bit)]
        else:
            pieces = []
            for low in reversed(range(1 << (bit - 2))):
                holders = [
                    i for i in range(count // 4) if i << 2 & ones == ones and not i << 2 >> bit & 1
                ]
                wanted = {i: (i & ~(ones >> 2)) | low | (1 << (bit - 2)) for i in holders}
                pairs = [(i * 4 + j, k * 4 + j) for i, k in spread(wanted, count // 4) for j in range(4)]
                pieces.append(lax.ppermute(running, "ctx", pairs))
        after = []
        for _ in range(2):
            if waiting:
                after.append(work(waiting[0], after[-1] if after else running))
        got = chosen(pieces[::-1], after) if len(pieces) > 1 else pieces[0]
        if bit + 1 < bits:
            running = merged([running, got], after + [early, far1])
        nears.append(got)
        fars.append(exchange(got, 1))
    late = exchange(packed(nears[1:] + fars[1:-1], []), 0)
    later = bits - 1
    other_nears = [(early, 0)] + [(late, i) for i in range(later)]
    after = [work(where, nears[-1]) for where in list(waiting)]
    out, token = across(near, local[near], nears, None)
    out, token = across(other_near, local[other_near], other_nears, out)
    last = merged(fars[-1:], after + [token])
    other_fars = [(early, 1)] + [(late, later + i) for i in range(later - 1)]
    other_fars.append(exchange(last, 0))
    out, _ = across(far, local[far], fars[:-1] + [last], out)
    return across(other_far, local[other_far], other_fars, out)[0]


def solution(mesh):
    placed = (P(None, ("groups", "ctx"), None), P(), P(None, None, ("groups", "ctx")), P())
    return jax.shard_map(
        on_device, mesh=mesh, in_specs=placed, out_specs=P(("groups", "ctx"), None), check_vma=False
    )
```
